1024 devices in a mesh: row: 32 (over z_lo, x), col: 32 (over z_hi, y, core).
Axes of the slice: x: 4, y: 4, z: 32 (z_hi: 4, z_lo: 8; z = z_hi * 8 + z_lo), core: 2. Of those that a mesh axis runs over, the one named last changes fastest.
Arguments:
- a_blocks: float32 [1024, 131072], P('row', 'col'), may hold values from -0.75 to 0.75
- b_blocks: float32 [1024, 131072], P('row', 'col'), may hold values from -6 to 6
- c_blocks: float32 [2048, 131072], P('row', 'col'), may hold values from -6 to 6
- stack_a: int32 [96, 2048], P('row', 'col'), may hold values from 0 to 31
- stack_b: int32 [96, 2048], P('row', 'col'), may hold values from 0 to 31
- stack_c: int32 [96, 2048], P('row', 'col'), may hold values from 0 to 63
- stack_len: int32 [96, 32], P('row', 'col'), may hold values from 8 to 64, as said below
Outputs:
- c_out: float32 [2048, 131072], P('row', 'col')
The draws below stay inside these ranges and needn't reach their ends.
Inputs may be any that keep to these rules, and one draw needn't show every extreme that they name: `stack_len`: each stack length lies between 8 and 64; panel (0, 0) has full stacks in every phase.
All inputs are finite; a program needn't handle non-finite values.
Results may differ from the reference program's by a relative error of at most 0.0003.
Values sent between devices are 32-bit elements; how exact they have to be, the bound alone decides.
A program may use at most 32 MiB of HBM per device.

```python
import jax
import jax.numpy as jnp
from jax import lax

BLK = 64
NAS = 32
NBS = 32
NCS = 64
STACK = 64
STEPS = 2
PHASES = 3
N_ROW = 32
N_COL = 32


def draw_stack_len(key, part):
    key = jax.random.fold_in(key, 11)
    shifts = jax.random.randint(key, (N_ROW * (STEPS + 1), N_COL), 0, 4)
    lengths = jnp.right_shift(jnp.full((N_ROW * (STEPS + 1), N_COL), STACK, jnp.int32), shifts.astype(jnp.int32))
    lengths = lengths.at[0:STEPS + 1, 0].set(STACK)
    return lengths.astype(jnp.int32)


def plant(values, key, smallest, largest):
    longest = values.shape.index(max(values.shape))
    spots = []
    for shift in (0, 1):
        where = [jax.random.randint(jax.random.fold_in(key, axis), (), 0, length) for axis, length in enumerate(values.shape)]
        where[longest] = (where[longest] + shift) % values.shape[longest]
        spots.append(tuple(where))
    return values.at[spots[0]].set(smallest).at[spots[1]].set(largest)


def steps_of(own_key, dims, shards, least, top_value):
    loudness = 1.0
    for position, shards_of in shards:
        steps = jax.random.uniform(jax.random.fold_in(jax.random.fold_in(own_key, 6), position), (shards_of,), jnp.float32, least / len(shards), top_value / len(shards))
        loudness = loudness * jnp.repeat(jnp.exp(steps), dims[position] // shards_of).reshape((-1,) + (1,) * (len(dims) - 1 - position))
    return loudness


def normal_values(own_key, extent, deviation, limit, pieces=(), kind=jnp.bfloat16):
    drawn = deviation * jax.random.normal(own_key, extent, jnp.float32)
    if pieces:
        drawn = drawn * steps_of(own_key, extent, pieces, -0.22, 0.18)
    return jnp.clip(drawn, -limit, limit).astype(kind)


def setup_inputs(seed: int = 0) -> dict:
    key_list = jax.random.split(jax.random.key(seed), 8)
    a_blocks = normal_values(key_list[0], (N_ROW * NAS, N_COL * BLK * BLK), BLK ** -0.5, 0.75, ((0, 32), (1, 32)), jnp.float32)
    b_blocks = normal_values(key_list[1], (N_ROW * NBS, N_COL * BLK * BLK), 1.0, 6.0, ((0, 32), (1, 32)), jnp.float32)
    c_blocks = normal_values(key_list[2], (N_ROW * NCS, N_COL * BLK * BLK), 1.0, 6.0, ((0, 32), (1, 32)), jnp.float32)
    stack_a = plant(jax.random.randint(key_list[3], (N_ROW * PHASES, N_COL * STACK), 0, NAS), jax.random.fold_in(key_list[3], 1), 0, NAS - 1).astype(jnp.int32)
    stack_b = plant(jax.random.randint(key_list[4], (N_ROW * PHASES, N_COL * STACK), 0, NBS), jax.random.fold_in(key_list[4], 1), 0, NBS - 1).astype(jnp.int32)
    stack_c = plant(jax.random.randint(key_list[5], (N_ROW * PHASES, N_COL * STACK), 0, NCS), jax.random.fold_in(key_list[5], 1), 0, NCS - 1).astype(jnp.int32)
    stack_len = draw_stack_len(jax.random.fold_in(key_list[7], 71), 0)
    return dict(a_blocks=a_blocks, b_blocks=b_blocks, c_blocks=c_blocks, stack_a=stack_a, stack_b=stack_b, stack_c=stack_c, stack_len=stack_len)


def reference(a_blocks, b_blocks, c_blocks, stack_a, stack_b, stack_c, stack_len):
    n_row = N_ROW
    n_col = N_COL
    phases = STEPS + 1
    a_four = a_blocks.reshape(n_row, NAS, n_col, BLK, BLK).transpose(0, 2, 1, 3, 4)
    b_four = b_blocks.reshape(n_row, NBS, n_col, BLK, BLK).transpose(0, 2, 1, 3, 4)
    c_four = c_blocks.reshape(n_row, NCS, n_col, BLK, BLK).transpose(0, 2, 1, 3, 4)
    sa_all = stack_a.reshape(n_row, phases, n_col, STACK).transpose(0, 2, 1, 3)
    sb_all = stack_b.reshape(n_row, phases, n_col, STACK).transpose(0, 2, 1, 3)
    sc_all = stack_c.reshape(n_row, phases, n_col, STACK).transpose(0, 2, 1, 3)
    len_all = stack_len.reshape(n_row, phases, n_col).transpose(0, 2, 1)
    slots = jnp.arange(STACK, dtype=jnp.int32)

    def one_row(index):
        total = c_four[index].astype(jnp.float32)
        for phase in range(phases):
            a_panels = jnp.roll(a_four[index], -phase, axis=0)
            b_panels = b_four[(index + phase) % n_row]
            picked_a = jax.vmap(lambda p, s: p[s])(a_panels, sa_all[index, :, phase])
            picked_b = jax.vmap(lambda p, s: p[s])(b_panels, sb_all[index, :, phase])
            product = jnp.einsum("jkab,jkbc->jkac", picked_a, picked_b, precision=lax.Precision.HIGHEST)
            live = (slots[None, :] < len_all[index, :, phase][:, None]).astype(jnp.float32)
            product = product * live[:, :, None, None]
            added = jax.vmap(lambda p, s: jax.ops.segment_sum(p, s, num_segments=NCS))(product, sc_all[index, :, phase])
            total = total + added
        return total

    result = lax.map(one_row, jnp.arange(n_row, dtype=jnp.int32))
    return result.transpose(0, 2, 1, 3, 4).reshape(n_row * NCS, n_col * BLK * BLK)
```

```python
import functools

import jax
import jax.numpy as jnp
from jax import lax
from jax.experimental import pallas as pl
from jax.experimental.pallas import tpu as pltpu
from jax.sharding import PartitionSpec as P

MESH = pl.DeviceIdType.MESH
NX, NY, NZL, NZH = 4, 4, 8, 4
BLK = 64
LANES = 128
SUB = 8
PARTS = 4
F32, BF16 = jnp.float32, jnp.bfloat16


def on_left():
    return lax.broadcasted_iota(jnp.int32, (32, LANES), 1) < BLK


def halves(block):
    high = block.astype(BF16).astype(F32)
    rest = block - high
    left = on_left()
    even = jnp.where(left, high, pltpu.roll(rest, BLK, 1))
    odd = jnp.where(left, pltpu.roll(high, BLK, 1), rest)
    return even, odd


def split_a(panel, out, part):
    for s in range(SUB):
        even, odd = halves(panel[pl.ds(part * 256 + s, 32, stride=SUB), :])
        out[part * SUB + s, 0:32, :] = even.astype(BF16)
        out[part * SUB + s, 32:64, :] = odd.astype(BF16)


def split_b(panel, out, mixed, part):
    for s in range(SUB):
        even, odd = halves(panel[pl.ds(part * 256 + s, 32, stride=SUB), :])
        mixed[s, pl.ds(0, 32, stride=2), :] = even
        mixed[s, pl.ds(1, 32, stride=2), :] = odd
        out[part * SUB + s] = mixed[s].astype(BF16)


def multiply(phase, groups, sa_ref, sb_ref, fa, fb, prods):
    left = on_left()

    def body(g, carry):
        for s in range(SUB):
            e = g * SUB + s
            a = fa[sa_ref[phase, e]]
            b = fb[sb_ref[phase, e]]
            both = jnp.dot(a, jnp.concatenate([b, b], axis=0), preferred_element_type=F32)
            whole = both + pltpu.roll(both, BLK, 1)
            prods[pl.ds(g * 256 + s, 32, stride=SUB), :] = jnp.where(left, whole[0:32], whole[32:64])
        return carry

    lax.fori_loop(groups[0], groups[1], body, 0)


def spread(prods, spots, acc):
    def body(h, carry):
        for u in range(4):
            t = h * 4 + u
            rows = [prods[pl.ds(g * 256 + t * SUB, SUB), :] for g in range(8)]
            x = jnp.concatenate(rows, axis=0)
            high = x.astype(BF16)
            rest = (x - high.astype(F32)).astype(BF16)
            add = jnp.dot(spots, jnp.concatenate([high, rest], axis=0), preferred_element_type=F32)
            at = pl.ds(pl.multiple_of(t * LANES, LANES), LANES)
            acc[:, at] = acc[:, at] + add
        return carry

    lax.fori_loop(0, 8, body, 0)


def kernel(sa_ref, sb_ref, sl_ref, sc_ref, a_hbm, b_hbm, c_hbm, out_hbm,
           a_own, b_own, acc, a_next, a_side, b_one, b_two, relay, fa, fb, mixed, prods, spot,
           own_sem, a_send, a_recv, side_send, side_recv, b_send, b_recv, b2_send, b2_recv,
           rel_send, rel_recv, far_send, far_ok, wrap_ok):
    row, col = lax.axis_index("row"), lax.axis_index("col")
    x, zl = lax.rem(row, NX), lax.div(row, NX)
    core, y, zh = lax.rem(col, 2), lax.rem(lax.div(col, 2), NY), lax.div(col, 2 * NY)

    def at(y_, zh_):
        return (row, (lax.rem(zh_ + NZH, NZH) * NY + y_) * 2 + core)

    other = (row, col + 1 - 2 * core)
    up = (lax.rem(row + NX * NZL - 1, NX * NZL), col)
    down = (lax.rem(row + 1, NX * NZL), col)
    far = at(3, zh - 1)
    first_zh, last_zh = zh == 0, zh == NZH - 1
    wrap_from = row == 0
    wrap_to = row == NX * NZL - 1

    own = [
        pltpu.make_async_copy(a_hbm, a_own, own_sem.at[0]),
        pltpu.make_async_copy(b_hbm, b_own, own_sem.at[1]),
        pltpu.make_async_copy(c_hbm, acc, own_sem.at[2]),
    ]
    for copy in own:
        copy.start()

    barrier = pltpu.get_barrier_semaphore()

    def greet(device):
        pl.semaphore_signal(barrier, inc=1, device_id=device, device_id_type=MESH)

    @pl.when((y == 3) & jnp.logical_not(last_zh))
    def _():
        for k in range(NY):
            greet(at(k, zh + 1))

    @pl.when(first_zh)
    def _():
        greet(far)

    @pl.when(y >= 1)
    def _():
        greet(at(0, zh))

    @pl.when(y <= 2)
    def _():
        greet(at(y + 1, zh))

    greet(other)

    @pl.when(jnp.logical_not(wrap_to))
    def _():
        greet(down)

    @pl.when(wrap_from)
    def _():
        greet(up)

    expected = (1 + jnp.where(wrap_from, 0, 1) + jnp.where(wrap_to, 1, 0) + jnp.where(y == 0, 3, 1)
                + jnp.where(first_zh, 0, 1) + jnp.where((y == 3) & last_zh, NY, 0))
    pl.semaphore_wait(barrier, expected)

    @pl.when((y == 3) & last_zh)
    def _():
        for k in range(NY):
            pl.semaphore_signal(far_ok, inc=1, device_id=at(k, zh + 1), device_id_type=MESH)

    @pl.when(wrap_to)
    def _():
        pl.semaphore_signal(wrap_ok, inc=1, device_id=down, device_id_type=MESH)

    def quarter(ref, q):
        return ref.at[pl.ds(q * 256, 256)]

    def a_copy(q, device):
        return pltpu.make_async_remote_copy(quarter(a_hbm, q), quarter(a_next, q), a_send.at[q], a_recv.at[q],
                                            device_id=device, device_id_type=MESH)

    def relay_copy(q):
        return pltpu.make_async_remote_copy(quarter(a_hbm, q), relay, rel_send.at[q], rel_recv,
                                            device_id=at(q, zh), device_id_type=MESH)

    def far_copy(q):
        return pltpu.make_async_remote_copy(relay, quarter(a_next, q), far_send, a_recv.at[q],
                                            device_id=far, device_id_type=MESH)

    def side_copy(q, source):
        return pltpu.make_async_remote_copy(quarter(source, q), quarter(a_side, q), side_send.at[q], side_recv.at[q],
                                            device_id=other, device_id_type=MESH)

    def b_copy(q):
        return pltpu.make_async_remote_copy(quarter(b_hbm, q), quarter(b_one, q), b_send.at[q], b_recv.at[q],
                                            device_id=up, device_id_type=MESH)

    def b2_copy(q):
        return pltpu.make_async_remote_copy(quarter(b_one, q), quarter(b_two, q), b2_send.at[q], b2_recv.at[q],
                                            device_id=up, device_id_type=MESH)

    @pl.when(y == 0)
    def _():
        for q in (2, 1, 3):
            relay_copy(q).start()

        @pl.when(jnp.logical_not(first_zh))
        def _():
            a_copy(0, far).start()

    @pl.when(y >= 1)
    def _():
        for q in range(PARTS):
            a_copy(q, at(y - 1, zh)).start()

    @pl.when(jnp.logical_not(wrap_from))
    def _():
        for q in range(PARTS):
            b_copy(q).start()

    @pl.when(core == 1)
    def _():
        for q in range(PARTS):
            side_copy(q, a_hbm).start()

    def mark(phase):
        slot = lax.broadcasted_iota(jnp.int32, (BLK, BLK), 0)
        entry = lax.broadcasted_iota(jnp.int32, (BLK, BLK), 1)
        hit = (slot == sc_ref[phase:phase + 1, :]) & (entry < sl_ref[phase, 0])
        ones = jnp.where(hit, 1.0, 0.0)
        spot[:, 0:BLK] = ones
        spot[:, BLK:LANES] = ones

    def forward_relay():
        for q in range(1, PARTS):
            @pl.when(y == q)
            def _():
                relay_copy(q).wait_recv()
                far_copy(q).start()

    own[0].wait()
    for q in range(2):
        split_a(a_own, fa, q)

    @pl.when(jnp.logical_not(first_zh))
    def _():
        forward_relay()

    for q in range(2, PARTS):
        split_a(a_own, fa, q)
    own[1].wait()
    for q in range(PARTS):
        split_b(b_own, fb, mixed, q)
    mark(0)

    @pl.when(wrap_from)
    def _():
        pl.semaphore_wait(wrap_ok, 1)
        for q in range(PARTS):
            b_copy(q).start()

    for q in range(PARTS):
        multiply(0, (2 * q, 2 * q + 2), sa_ref, sb_ref, fa, fb, prods)
        b_copy(q).wait_recv()
        b2_copy(q).start()

    own[2].wait()
    spread(prods, spot[...].astype(BF16), acc)

    @pl.when(first_zh)
    def _():
        pl.semaphore_wait(far_ok, 1)

        @pl.when(y == 0)
        def _():
            a_copy(0, far).start()

        forward_relay()

    mark(1)
    for q in range(PARTS):
        split_b(b_one, fb, mixed, q)
    for q in range(PARTS):
        side_copy(q, a_hbm).wait_recv()
        split_a(a_side, fa, q)
    multiply(1, (0, 8), sa_ref, sb_ref, fa, fb, prods)
    spread(prods, spot[...].astype(BF16), acc)

    mark(2)
    for q in range(PARTS):
        b2_copy(q).wait_recv()
        split_b(b_two, fb, mixed, q)
    for q in range(PARTS):
        a_copy(q, far).wait_recv()

        @pl.when(core == 0)
        def _():
            side_copy(q, a_next).start()

    for q in range(PARTS):
        split_a(a_next, fa, q)
    multiply(2, (0, 8), sa_ref, sb_ref, fa, fb, prods)
    spread(prods, spot[...].astype(BF16), acc)
    result = pltpu.make_async_copy(acc, out_hbm, own_sem.at[0])
    result.start()

    for q in range(PARTS):
        side_copy(q, a_hbm).wait_send()
        b_copy(q).wait_send()
        b2_copy(q).wait_send()

    @pl.when(y == 0)
    def _():
        a_copy(0, far).wait_send()
        for q in (1, 2, 3):
            relay_copy(q).wait_send()

    @pl.when(y >= 1)
    def _():
        far_copy(0).wait_send()
        for q in range(PARTS):
            a_copy(q, far).wait_send()

    result.wait()


def tiles(panel):
    rows, cols = panel.shape
    view = panel.reshape(rows // SUB, SUB, cols // LANES, LANES).transpose(0, 2, 1, 3)
    return view.reshape(rows * cols // LANES, LANES)


def on_device(a_blocks, b_blocks, c_blocks, stack_a, stack_b, stack_c, stack_len):
    smem = pl.BlockSpec(memory_space=pltpu.SMEM)
    vmem = pl.BlockSpec(memory_space=pltpu.VMEM)
    hbm = pl.BlockSpec(memory_space=pl.ANY)
    panel = pltpu.VMEM((1024, LANES), F32)
    dma = pltpu.SemaphoreType.DMA
    return pl.pallas_call(
        kernel,
        out_shape=jax.ShapeDtypeStruct(c_blocks.shape, F32),
        in_specs=[smem, smem, smem, vmem, hbm, hbm, hbm],
        out_specs=hbm,
        scratch_shapes=[
            panel, panel, pltpu.VMEM((64, 4096), F32), panel, panel, panel, panel,
            pltpu.VMEM((256, LANES), F32),
            pltpu.VMEM((32, BLK, LANES), BF16), pltpu.VMEM((32, BLK, LANES), BF16),
            pltpu.VMEM((SUB, BLK, LANES), F32), pltpu.VMEM((2048, LANES), F32), pltpu.VMEM((BLK, LANES), F32),
            dma((3,)), dma((4,)), dma((4,)), dma((4,)), dma((4,)), dma((4,)), dma((4,)), dma((4,)), dma((4,)),
            dma((4,)), dma, dma, pltpu.SemaphoreType.REGULAR, pltpu.SemaphoreType.REGULAR,
        ],
        compiler_params=pltpu.CompilerParams(collective_id=0, has_side_effects=True, vmem_limit_bytes=32 * 2 ** 20),
        cost_estimate=pl.CostEstimate(flops=300_000_000, bytes_accessed=4_000_000, transcendentals=0),
    )(stack_a, stack_b, stack_len, stack_c, tiles(a_blocks), tiles(b_blocks), c_blocks)


def solution(mesh):
    placed = P("row", "col")
    return jax.shard_map(
        on_device, mesh=mesh, in_specs=(placed,) * 7, out_specs=placed, check_vma=False
    )
```

```python
import functools

import jax
import jax.numpy as jnp
from jax import lax
from jax.experimental import pallas as pl
from jax.experimental.pallas import tpu as pltpu
from jax.sharding import PartitionSpec as P

MESH = pl.DeviceIdType.MESH
NX, NY, NZL, NZH = 4, 4, 8, 4
BLK = 64
LANES = 128
SUB = 8
PARTS = 4
F32, BF16 = jnp.float32, jnp.bfloat16


def on_left():
    return lax.broadcasted_iota(jnp.int32, (32, LANES), 1) < BLK


def halves(block):
    high = block.astype(BF16).astype(F32)
    rest = block - high
    left = on_left()
    even = jnp.where(left, high, pltpu.roll(rest, BLK, 1))
    odd = jnp.where(left, pltpu.roll(high, BLK, 1), rest)
    return even, odd


def split_a(panel, out, part):
    for s in range(SUB):
        even, odd = halves(panel[pl.ds(part * 256 + s, 32, stride=SUB), :])
        out[part * SUB + s, 0:32, :] = even.astype(BF16)
        out[part * SUB + s, 32:64, :] = odd.astype(BF16)


def split_b(panel, out, mixed, part):
    for s in range(SUB):
        even, odd = halves(panel[pl.ds(part * 256 + s, 32, stride=SUB), :])
        mixed[s, pl.ds(0, 32, stride=2), :] = even
        mixed[s, pl.ds(1, 32, stride=2), :] = odd
        out[part * SUB + s] = mixed[s].astype(BF16)


def multiply(phase, first, groups, sa_ref, sb_ref, fa, fb, prods):
    left = on_left()

    def body(h, carry):
        for n in range(2 * SUB):
            g, s = h * 2 + n // SUB, n % SUB
            e = g * SUB + s
            a = fa[sa_ref[phase, e]]
            b = fb[sb_ref[phase, e]]
            both = jnp.dot(a, jnp.concatenate([b, b], axis=0), preferred_element_type=F32)
            whole = both + pltpu.roll(both, BLK, 1)
            prods[pl.ds(first + g * 256 + s, 32, stride=SUB), :] = jnp.where(left, whole[0:32], whole[32:64])
        return carry

    lax.fori_loop(groups[0] // 2, groups[1] // 2, body, 0)


def spread(prods, groups, spots, acc):
    def body(h, carry):
        for u in range(4):
            t = h * 4 + u
            rows = [prods[pl.ds(g * 256 + t * SUB, SUB), :] for g in range(groups)]
            x = jnp.concatenate(rows, axis=0)
            high = x.astype(BF16)
            rest = (x - high.astype(F32)).astype(BF16)
            add = jnp.dot(spots, jnp.concatenate([high, rest], axis=0), preferred_element_type=F32)
            at = pl.ds(pl.multiple_of(t * LANES, LANES), LANES)
            acc[:, at] = acc[:, at] + add
        return carry

    lax.fori_loop(0, 8, body, 0)


def kernel(sa_hbm, sb_hbm, sl_hbm, sc_hbm, a_hbm, b_hbm, c_hbm, acc,
           a_own, b_own, a_next, a_side, b_one, b_two, a_relay, b_relay, fa, fb, fa_two, fb_two, mixed, prods, spot,
           sa_ref, sb_ref, sl_ref, sc_ref,
           own_sem, a_send, a_recv, side_send, side_recv, b_send, b_recv, b2_send, b2_recv,
           rel_send, rel_recv, far_send, brel_send, brel_recv, bfar_send, far_ok, wrap_ok):
    row, col = lax.axis_index("row"), lax.axis_index("col")
    x, zl = lax.rem(row, NX), lax.div(row, NX)
    core, y, zh = lax.rem(col, 2), lax.rem(lax.div(col, 2), NY), lax.div(col, 2 * NY)

    def at(y_, zh_):
        return (row, (lax.rem(zh_ + NZH, NZH) * NY + y_) * 2 + core)

    def beside(x_, zl_):
        return (lax.rem(zl_ + NZL, NZL) * NX + x_, col)

    other = (row, col + 1 - 2 * core)
    far = at(3, zh - 1)
    above3, above2 = beside(3, zl - 1), beside(2, zl - 1)
    far_asks = (zh == 0) | (zh == NZH - 1)
    far_answers = (y == 3) & (zh >= NZH - 2)
    wrap_asks = zl == 0
    wrap_last = zl == NZL - 1

    sources = (sa_hbm, sb_hbm, sl_hbm, sc_hbm, a_hbm, b_hbm, c_hbm)
    places = (sa_ref, sb_ref, sl_ref, sc_ref, a_own, b_own, acc)
    own = [pltpu.make_async_copy(s_, d_, own_sem.at[n]) for n, (s_, d_) in enumerate(zip(sources, places))]

    barrier = pltpu.get_barrier_semaphore()

    def greet(device):
        pl.semaphore_signal(barrier, inc=1, device_id=device, device_id_type=MESH)

    @pl.when(far_asks)
    def _():
        greet(far)

    @pl.when(wrap_asks)
    def _():
        greet(above3)

        @pl.when(x != 1)
        def _():
            greet(above2)

    @pl.when((y == 3) & (zh < NZH - 2))
    def _():
        for k in range(NY):
            greet(at(k, zh + 1))

    @pl.when(y >= 1)
    def _():
        greet(at(0, zh))

    @pl.when(y <= 2)
    def _():
        greet(at(y + 1, zh))

    greet(other)

    for here, there in ((0, (1, 2)), (1, (2, 3)), (2, (3, 0, 1)), (3, (0,))):
        @pl.when(x == here)
        def _():
            for k in there:
                greet(beside(k, zl))

    for here, there in ((2, (0, 2, 3)), (3, (0, 1, 2, 3))):
        @pl.when((x == here) & jnp.logical_not(wrap_last))
        def _():
            for k in there:
                greet(beside(k, zl + 1))

    for copy in own[4:6] + own[:4] + own[6:]:
        copy.start()

    expected = (jnp.where(y == 0, 4, 2) + 2 + jnp.where(wrap_asks, 0, jnp.where(x == 1, 1, 2))
                + jnp.where(far_asks, 0, 1) + jnp.where(far_answers, NY, 0)
                + jnp.where(wrap_last, jnp.where(x == 3, 4, jnp.where(x == 2, 3, 0)), 0))
    pl.semaphore_wait(barrier, expected)

    @pl.when(far_answers)
    def _():
        for k in range(NY):
            pl.semaphore_signal(far_ok, inc=1, device_id=at(k, zh + 1), device_id_type=MESH)

    for here, there in ((2, (0, 2, 3)), (3, (0, 1, 2, 3))):
        @pl.when((x == here) & wrap_last)
        def _():
            for k in there:
                pl.semaphore_signal(wrap_ok, inc=1, device_id=beside(k, zl + 1), device_id_type=MESH)

    def quarter(ref, q):
        return ref.at[pl.ds(q * 256, 256)]

    def half(ref, q, h):
        return ref.at[pl.ds(q * 256 + h * 128, 128)]

    def send(source, target, send_sem, recv_sem, device):
        return pltpu.make_async_remote_copy(source, target, send_sem, recv_sem, device_id=device, device_id_type=MESH)

    def a_copy(q, h, device):
        return send(half(a_hbm, q, h), half(a_next, q, h), a_send.at[q, h], a_recv.at[q, h], device)

    def relay_copy(q, h):
        return send(half(a_hbm, q, h), half(a_relay, 0, h), rel_send.at[q, h], rel_recv.at[h], at(q, zh))

    def far_copy(q, h):
        return send(half(a_relay, 0, h), half(a_next, q, h), far_send.at[h], a_recv.at[q, h], far)

    def side_copy(q, source):
        return send(quarter(source, q), quarter(a_side, q), side_send.at[q], side_recv.at[q], other)

    def b_copy(q, device):
        return send(quarter(b_hbm, q), quarter(b_one, q), b_send.at[q], b_recv.at[q], device)

    def b2_copy(q, device):
        return send(quarter(b_hbm, q), quarter(b_two, q), b2_send.at[q], b2_recv.at[q], device)

    def b_relay_copy(q, slot, sem, device):
        return send(quarter(b_hbm, q), quarter(b_relay, slot), brel_send.at[sem], brel_recv.at[slot], device)

    def b_far_copy(sem, slot, q, target, recv, device):
        return send(quarter(b_relay, slot), quarter(target, q), bfar_send.at[sem], recv.at[q], device)

    @pl.when(y == 0)
    def _():
        for q in (2, 1, 3):
            for h in range(2):
                relay_copy(q, h).start()

    def send_above():
        @pl.when(x == 0)
        def _():
            b_copy(0, above3).start()
            b_copy(1, above3).start()
            b2_copy(0, above2).start()

        @pl.when(x == 1)
        def _():
            for q in range(3):
                b2_copy(q, above3).start()

    @pl.when(x == 0)
    def _():
        b_relay_copy(2, 1, 1, beside(3, zl)).start()
        b_relay_copy(3, 0, 2, beside(2, zl)).start()
        b_relay_copy(1, 0, 0, beside(3, zl)).start()

    @pl.when(x == 1)
    def _():
        b_relay_copy(3, 1, 0, beside(2, zl)).start()

    @pl.when(y >= 1)
    def _():
        for q in range(PARTS):
            for h in range(2):
                a_copy(q, h, at(y - 1, zh)).start()

    @pl.when(x >= 1)
    def _():
        for q in range(PARTS):
            b_copy(q, beside(x - 1, zl)).start()

    @pl.when(x >= 2)
    def _():
        for q in range(PARTS):
            b2_copy(q, beside(x - 2, zl)).start()

    @pl.when(core == 1)
    def _():
        for q in range(PARTS):
            side_copy(q, a_hbm).start()

    def forward_above():
        @pl.when(x == 2)
        def _():
            b_relay_copy(3, 0, 0, above3).wait_recv()
            b_far_copy(0, 0, 3, b_one, b_recv, above3).start()
            b_far_copy(1, 0, 3, b_two, b2_recv, above2).start()
            b_relay_copy(3, 1, 0, above3).wait_recv()
            b_far_copy(2, 1, 3, b_two, b2_recv, above3).start()

        @pl.when(x == 3)
        def _():
            b_relay_copy(2, 1, 0, above3).wait_recv()
            b_far_copy(1, 1, 2, b_one, b_recv, above3).start()
            b_far_copy(2, 1, 2, b_two, b2_recv, above2).start()
            b_relay_copy(1, 0, 0, above3).wait_recv()
            b_far_copy(0, 0, 1, b_two, b2_recv, above2).start()

    def far_start():
        @pl.when(far_asks)
        def _():
            pl.semaphore_wait(far_ok, 1)

        @pl.when(y == 0)
        def _():
            for h in range(2):
                a_copy(0, h, far).start()

        for q in range(1, PARTS):
            @pl.when(y == q)
            def _():
                for h in range(2):
                    relay_copy(q, h).wait_recv()
                    far_copy(q, h).start()

    def far_left():
        @pl.when(y == 0)
        def _():
            for h in range(2):
                a_copy(0, h, far).wait_send()

        @pl.when(y >= 1)
        def _():
            for h in range(2):
                far_copy(1, h).wait_send()

    def mark(phase, at_):
        slot = lax.broadcasted_iota(jnp.int32, (BLK, BLK), 0)
        entry = lax.broadcasted_iota(jnp.int32, (BLK, BLK), 1)
        hit = (slot == sc_ref[phase:phase + 1, :]) & (entry < sl_ref[0, phase])
        ones = jnp.where(hit, 1.0, 0.0)
        spot[:, at_:at_ + BLK] = ones

    @pl.when(jnp.logical_not(far_asks))
    def _():
        far_start()

    own[4].wait()
    for q in range(PARTS):
        split_a(a_own, fa, q)
    own[5].wait()
    for q in range(PARTS):
        split_b(b_own, fb, mixed, q)

    for copy in own[:4]:
        copy.wait()
    mark(0, 0)
    mark(0, BLK)
    multiply(0, 0, (0, 8), sa_ref, sb_ref, fa, fb, prods)
    own[6].wait()
    spread(prods, 8, spot[:, 0:LANES].astype(BF16), acc)

    @pl.when(wrap_asks)
    def _():
        pl.semaphore_wait(wrap_ok, jnp.where(x == 1, 1, 2))

    send_above()
    forward_above()

    @pl.when(far_asks)
    def _():
        far_start()


    for n in range(2):
        mark(1, n * LANES)
        mark(2, n * LANES + BLK)
    for q in range(PARTS):
        b_copy(q, other).wait_recv()
        split_b(b_one, fb, mixed, q)

    def phase_one():
        for q in range(PARTS):
            side_copy(q, a_hbm).wait_recv()
            split_a(a_side, fa, q)
        multiply(1, 0, (0, 8), sa_ref, sb_ref, fa, fb, prods)

    @pl.when(core == 0)
    def _():
        phase_one()

    for q in range(PARTS):
        b2_copy(q, other).wait_recv()
        split_b(b_two, fb_two, mixed, q)
    for q in range(PARTS):
        for h in range(2):
            a_copy(q, h, far).wait_recv()

        @pl.when(core == 0)
        def _():
            side_copy(q, a_next).start()

        split_a(a_next, fa_two, q)
    multiply(2, 2048, (0, 8), sa_ref, sb_ref, fa_two, fb_two, prods)

    @pl.when(core == 1)
    def _():
        phase_one()

    spread(prods, 16, spot[...].astype(BF16), acc)

    far_left()

    for q in range(PARTS):
        side_copy(q, a_hbm).wait_send()

    @pl.when(y == 0)
    def _():
        for q in (1, 2, 3):
            for h in range(2):
                relay_copy(q, h).wait_send()

    @pl.when(y >= 1)
    def _():
        for q in range(PARTS):
            for h in range(2):
                a_copy(q, h, far).wait_send()

    @pl.when(x == 0)
    def _():
        b_copy(0, other).wait_send()
        b_copy(1, other).wait_send()
        b2_copy(0, other).wait_send()
        for sem in range(3):
            b_relay_copy(0, 0, sem, other).wait_send()

    @pl.when(x >= 1)
    def _():
        for q in range(PARTS):
            b_copy(q, other).wait_send()
        for q in range(3):
            b2_copy(q, other).wait_send()

    @pl.when(x == 1)
    def _():
        b_relay_copy(0, 0, 0, other).wait_send()

    @pl.when(x >= 2)
    def _():
        b2_copy(3, other).wait_send()
        for sem in range(3):
            b_far_copy(sem, 0, 0, b_one, b_recv, other).wait_send()


def tiles(panel):
    rows, cols = panel.shape
    view = panel.reshape(rows // SUB, SUB, cols // LANES, LANES).transpose(0, 2, 1, 3)
    return view.reshape(rows * cols // LANES, LANES)


def on_device(a_blocks, b_blocks, c_blocks, stack_a, stack_b, stack_c, stack_len):
    hbm = pl.BlockSpec(memory_space=pl.ANY)
    panel = pltpu.VMEM((1024, LANES), F32)
    split = pltpu.VMEM((32, BLK, LANES), BF16)
    dma, flag = pltpu.SemaphoreType.DMA, pltpu.SemaphoreType.REGULAR
    picks = pltpu.SMEM(stack_a.shape, jnp.int32)
    return pl.pallas_call(
        kernel,
        out_shape=jax.ShapeDtypeStruct(c_blocks.shape, F32),
        in_specs=[hbm] * 7,
        out_specs=pl.BlockSpec(memory_space=pltpu.VMEM),
        scratch_shapes=[
            panel, panel, panel, panel, panel, panel, pltpu.VMEM((256, LANES), F32), pltpu.VMEM((512, LANES), F32),
            split, split, split, split,
            pltpu.VMEM((SUB, BLK, LANES), F32), pltpu.VMEM((4096, LANES), F32), pltpu.VMEM((BLK, 2 * LANES), F32),
            picks, picks, pltpu.SMEM(stack_len.shape[::-1], jnp.int32), pltpu.VMEM(stack_c.shape, jnp.int32),
            dma((7,)), dma((4, 2)), dma((4, 2)), dma((4,)), dma((4,)), dma((4,)), dma((4,)), dma((4,)), dma((4,)),
            dma((4, 2)), dma((2,)), dma((2,)), dma((3,)), dma((2,)), dma((3,)), flag, flag,
        ],
        compiler_params=pltpu.CompilerParams(collective_id=0, has_side_effects=True, vmem_limit_bytes=56 * 2 ** 20),
        cost_estimate=pl.CostEstimate(flops=300_000_000, bytes_accessed=4_000_000, transcendentals=0),
    )(stack_a, stack_b, stack_len.T, stack_c, tiles(a_blocks), tiles(b_blocks), c_blocks)


def solution(mesh):
    placed = P("row", "col")
    return jax.shard_map(
        on_device, mesh=mesh, in_specs=(placed,) * 7, out_specs=placed, check_vma=False
    )
```

```python
import functools

import jax
import jax.numpy as jnp
from jax import lax
from jax.experimental import pallas as pl
from jax.experimental.pallas import tpu as pltpu
from jax.sharding import PartitionSpec as P

MESH = pl.DeviceIdType.MESH
NX, NY, NZL, NZH = 4, 4, 8, 4
BLK = 64
LANES = 128
SUB = 8
PARTS = 4
F32, BF16 = jnp.float32, jnp.bfloat16


def on_left():
    return lax.broadcasted_iota(jnp.int32, (32, LANES), 1) < BLK


def halves(block):
    high = block.astype(BF16).astype(F32)
    rest = block - high
    left = on_left()
    even = jnp.where(left, high, pltpu.roll(rest, BLK, 1))
    odd = jnp.where(left, pltpu.roll(high, BLK, 1), rest)
    return even, odd


def split_a(panel, out, part):
    for s in range(SUB):
        even, odd = halves(panel[pl.ds(part * 256 + s, 32, stride=SUB), :])
        out[part * SUB + s, 0:32, :] = even.astype(BF16)
        out[part * SUB + s, 32:64, :] = odd.astype(BF16)


def split_b(panel, out, mixed, part):
    for s in range(SUB):
        even, odd = halves(panel[pl.ds(part * 256 + s, 32, stride=SUB), :])
        mixed[s, pl.ds(0, 32, stride=2), :] = even
        mixed[s, pl.ds(1, 32, stride=2), :] = odd
        out[part * SUB + s] = mixed[s].astype(BF16)


def multiply(phase, first, wide, sa_ref, sb_ref, fa, fb, prods):
    left = on_left()

    def body(h, carry):
        for n in range(wide * SUB):
            g, s = h * wide + n // SUB, n % SUB
            e = g * SUB + s
            a = fa[sa_ref[phase, e]]
            b = fb[sb_ref[phase, e]]
            both = jnp.dot(a, jnp.concatenate([b, b], axis=0), preferred_element_type=F32)
            whole = both + pltpu.roll(both, BLK, 1)
            prods[pl.ds(first + g * 256 + s, 32, stride=SUB), :] = jnp.where(left, whole[0:32], whole[32:64])
        return carry

    lax.fori_loop(0, 8 // wide, body, 0)


def spread(prods, groups, wide, spots, acc):
    def body(h, carry):
        for u in range(wide):
            t = h * wide + u
            rows = [prods[pl.ds(g * 256 + t * SUB, SUB), :] for g in range(groups)]
            x = jnp.concatenate(rows, axis=0)
            high = x.astype(BF16)
            rest = (x - high.astype(F32)).astype(BF16)
            add = jnp.dot(spots, jnp.concatenate([high, rest], axis=0), preferred_element_type=F32)
            at = pl.ds(pl.multiple_of(t * LANES, LANES), LANES)
            acc[:, at] = acc[:, at] + add
        return carry

    lax.fori_loop(0, 32 // wide, body, 0)


def kernel(sa_hbm, sb_hbm, sl_hbm, sc_hbm, a_hbm, b_hbm, c_hbm, acc,
           a_own, b_own, a_next, a_side, b_one, b_two, a_relay, b_relay, fa, fb, fa_two, fb_two, mixed, prods, spot,
           sa_ref, sb_ref, sl_ref, sc_ref,
           own_sem, a_send, a_recv, side_send, side_recv, b_send, b_recv, b2_send, b2_recv,
           rel_send, rel_recv, far_send, brel_send, brel_recv, bfar_send, far_ok, wrap_ok):
    row, col = lax.axis_index("row"), lax.axis_index("col")
    x, zl = lax.rem(row, NX), lax.div(row, NX)
    core, y, zh = lax.rem(col, 2), lax.rem(lax.div(col, 2), NY), lax.div(col, 2 * NY)

    def at(y_, zh_):
        return (row, (lax.rem(zh_ + NZH, NZH) * NY + y_) * 2 + core)

    def beside(x_, zl_):
        return (lax.rem(zl_ + NZL, NZL) * NX + x_, col)

    other = (row, col + 1 - 2 * core)
    far = at(3, zh - 1)
    above3, above2 = beside(3, zl - 1), beside(2, zl - 1)
    far_asks = (zh == 0) | (zh == NZH - 1)
    far_answers = (y == 3) & (zh >= NZH - 2)
    wrap_asks = zl == 0
    wrap_last = zl == NZL - 1

    sources = (sa_hbm, sb_hbm, sl_hbm, sc_hbm, a_hbm, b_hbm, c_hbm)
    places = (sa_ref, sb_ref, sl_ref, sc_ref, a_own, b_own, acc)
    own = [pltpu.make_async_copy(s_, d_, own_sem.at[n]) for n, (s_, d_) in enumerate(zip(sources, places))]

    barrier = pltpu.get_barrier_semaphore()

    def greet(device):
        pl.semaphore_signal(barrier, inc=1, device_id=device, device_id_type=MESH)

    @pl.when(far_asks)
    def _():
        greet(far)

    @pl.when(wrap_asks)
    def _():
        greet(above3)

        @pl.when(x != 1)
        def _():
            greet(above2)

    @pl.when((y == 3) & (zh < NZH - 2))
    def _():
        for k in range(NY):
            greet(at(k, zh + 1))

    @pl.when(y >= 1)
    def _():
        greet(at(0, zh))

    @pl.when(y <= 2)
    def _():
        greet(at(y + 1, zh))

    greet(other)

    for here, there in ((0, (1, 2)), (1, (2, 3)), (2, (3, 0, 1)), (3, (0,))):
        @pl.when(x == here)
        def _():
            for k in there:
                greet(beside(k, zl))

    for here, there in ((2, (0, 2, 3)), (3, (0, 1, 2, 3))):
        @pl.when((x == here) & jnp.logical_not(wrap_last))
        def _():
            for k in there:
                greet(beside(k, zl + 1))

    for copy in own[4:6] + own[:4] + own[6:]:
        copy.start()

    expected = (jnp.where(y == 0, 4, 2) + 2 + jnp.where(wrap_asks, 0, jnp.where(x == 1, 1, 2))
                + jnp.where(far_asks, 0, 1) + jnp.where(far_answers, NY, 0)
                + jnp.where(wrap_last, jnp.where(x == 3, 4, jnp.where(x == 2, 3, 0)), 0))
    pl.semaphore_wait(barrier, expected)

    @pl.when(far_answers)
    def _():
        for k in range(NY):
            pl.semaphore_signal(far_ok, inc=1, device_id=at(k, zh + 1), device_id_type=MESH)

    for here, there in ((2, (0, 2, 3)), (3, (0, 1, 2, 3))):
        @pl.when((x == here) & wrap_last)
        def _():
            for k in there:
                pl.semaphore_signal(wrap_ok, inc=1, device_id=beside(k, zl + 1), device_id_type=MESH)

    def quarter(ref, q):
        return ref.at[pl.ds(q * 256, 256)]

    def half(ref, q, h):
        return ref.at[pl.ds(q * 256 + h * 128, 128)]

    def send(source, target, send_sem, recv_sem, device):
        return pltpu.make_async_remote_copy(source, target, send_sem, recv_sem, device_id=device, device_id_type=MESH)

    def a_copy(q, h, device):
        return send(half(a_hbm, q, h), half(a_next, q, h), a_send.at[q, h], a_recv.at[q, h], device)

    def relay_copy(q, h):
        return send(half(a_hbm, q, h), half(a_relay, 0, h), rel_send.at[q, h], rel_recv.at[h], at(q, zh))

    def far_copy(q, h):
        return send(half(a_relay, 0, h), half(a_next, q, h), far_send.at[h], a_recv.at[q, h], far)

    def side_copy(q, source):
        return send(quarter(source, q), quarter(a_side, q), side_send.at[q], side_recv.at[q], other)

    def b_copy(q, device):
        return send(quarter(b_hbm, q), quarter(b_one, q), b_send.at[q], b_recv.at[q], device)

    def b2_copy(q, device):
        return send(quarter(b_hbm, q), quarter(b_two, q), b2_send.at[q], b2_recv.at[q], device)

    def b_relay_copy(q, slot, sem, device):
        return send(quarter(b_hbm, q), quarter(b_relay, slot), brel_send.at[sem], brel_recv.at[slot], device)

    def b_far_copy(sem, slot, q, target, recv, device):
        return send(quarter(b_relay, slot), quarter(target, q), bfar_send.at[sem], recv.at[q], device)

    @pl.when(y == 0)
    def _():
        for q in (2, 1, 3):
            for h in range(2):
                relay_copy(q, h).start()

    def send_above():
        @pl.when(x == 0)
        def _():
            b_copy(0, above3).start()
            b_copy(1, above3).start()
            b2_copy(0, above2).start()

        @pl.when(x == 1)
        def _():
            for q in range(3):
                b2_copy(q, above3).start()

    @pl.when(x == 0)
    def _():
        b_relay_copy(2, 1, 1, beside(3, zl)).start()
        b_relay_copy(3, 0, 2, beside(2, zl)).start()
        b_relay_copy(1, 0, 0, beside(3, zl)).start()

    @pl.when(x == 1)
    def _():
        b_relay_copy(3, 1, 0, beside(2, zl)).start()

    @pl.when(y >= 1)
    def _():
        for q in range(PARTS):
            for h in range(2):
                a_copy(q, h, at(y - 1, zh)).start()

    @pl.when(x >= 1)
    def _():
        for q in range(PARTS):
            b_copy(q, beside(x - 1, zl)).start()

    @pl.when(x >= 2)
    def _():
        for q in range(PARTS):
            b2_copy(q, beside(x - 2, zl)).start()

    @pl.when(core == 1)
    def _():
        for q in range(PARTS):
            side_copy(q, a_hbm).start()

    def forward_above():
        @pl.when(x == 2)
        def _():
            b_relay_copy(3, 0, 0, above3).wait_recv()
            b_far_copy(0, 0, 3, b_one, b_recv, above3).start()
            b_far_copy(1, 0, 3, b_two, b2_recv, above2).start()
            b_relay_copy(3, 1, 0, above3).wait_recv()
            b_far_copy(2, 1, 3, b_two, b2_recv, above3).start()

        @pl.when(x == 3)
        def _():
            b_relay_copy(2, 1, 0, above3).wait_recv()
            b_far_copy(1, 1, 2, b_one, b_recv, above3).start()
            b_far_copy(2, 1, 2, b_two, b2_recv, above2).start()
            b_relay_copy(1, 0, 0, above3).wait_recv()
            b_far_copy(0, 0, 1, b_two, b2_recv, above2).start()

    def far_start():
        @pl.when(far_asks)
        def _():
            pl.semaphore_wait(far_ok, 1)

        @pl.when(y == 0)
        def _():
            for h in range(2):
                a_copy(0, h, far).start()

        for q in range(1, PARTS):
            @pl.when(y == q)
            def _():
                for h in range(2):
                    relay_copy(q, h).wait_recv()
                    far_copy(q, h).start()

    def far_left():
        @pl.when(y == 0)
        def _():
            for h in range(2):
                a_copy(0, h, far).wait_send()

        @pl.when(y >= 1)
        def _():
            for h in range(2):
                far_copy(1, h).wait_send()

    def mark(phase, at_):
        slot = lax.broadcasted_iota(jnp.int32, (BLK, BLK), 0)
        entry = lax.broadcasted_iota(jnp.int32, (BLK, BLK), 1)
        hit = (slot == sc_ref[phase:phase + 1, :]) & (entry < sl_ref[0, phase])
        ones = jnp.where(hit, 1.0, 0.0)
        spot[:, at_:at_ + BLK] = ones

    @pl.when(jnp.logical_not(far_asks))
    def _():
        far_start()

    own[4].wait()
    for q in range(PARTS):
        split_a(a_own, fa, q)
    own[5].wait()
    for q in range(PARTS):
        split_b(b_own, fb, mixed, q)

    for copy in own[:4]:
        copy.wait()
    mark(0, 0)
    mark(0, BLK)
    multiply(0, 0, 1, sa_ref, sb_ref, fa, fb, prods)
    own[6].wait()
    spread(prods, 8, 4, spot[:, 0:LANES].astype(BF16), acc)

    @pl.when(wrap_asks)
    def _():
        pl.semaphore_wait(wrap_ok, jnp.where(x == 1, 1, 2))

    send_above()
    forward_above()

    @pl.when(far_asks)
    def _():
        far_start()


    for n in range(2):
        mark(1, n * LANES)
        mark(2, n * LANES + BLK)
    for q in range(PARTS):
        b_copy(q, other).wait_recv()
        split_b(b_one, fb, mixed, q)

    def phase_one():
        for q in range(PARTS):
            side_copy(q, a_hbm).wait_recv()
            split_a(a_side, fa, q)
        multiply(1, 0, 4, sa_ref, sb_ref, fa, fb, prods)

    @pl.when(core == 0)
    def _():
        phase_one()

    for q in range(PARTS):
        b2_copy(q, other).wait_recv()
        split_b(b_two, fb_two, mixed, q)
    for q in range(PARTS):
        for h in range(2):
            a_copy(q, h, far).wait_recv()

        @pl.when(core == 0)
        def _():
            side_copy(q, a_next).start()

        split_a(a_next, fa_two, q)
    multiply(2, 2048, 4, sa_ref, sb_ref, fa_two, fb_two, prods)

    @pl.when(core == 1)
    def _():
        phase_one()

    spread(prods, 16, 16, spot[...].astype(BF16), acc)

    far_left()

    for q in range(PARTS):
        side_copy(q, a_hbm).wait_send()

    @pl.when(y == 0)
    def _():
        for q in (1, 2, 3):
            for h in range(2):
                relay_copy(q, h).wait_send()

    @pl.when(y >= 1)
    def _():
        for q in range(PARTS):
            for h in range(2):
                a_copy(q, h, far).wait_send()

    @pl.when(x == 0)
    def _():
        b_copy(0, other).wait_send()
        b_copy(1, other).wait_send()
        b2_copy(0, other).wait_send()
        for sem in range(3):
            b_relay_copy(0, 0, sem, other).wait_send()

    @pl.when(x >= 1)
    def _():
        for q in range(PARTS):
            b_copy(q, other).wait_send()
        for q in range(3):
            b2_copy(q, other).wait_send()

    @pl.when(x == 1)
    def _():
        b_relay_copy(0, 0, 0, other).wait_send()

    @pl.when(x >= 2)
    def _():
        b2_copy(3, other).wait_send()
        for sem in range(3):
            b_far_copy(sem, 0, 0, b_one, b_recv, other).wait_send()


def tiles(panel):
    rows, cols = panel.shape
    view = panel.reshape(rows // SUB, SUB, cols // LANES, LANES).transpose(0, 2, 1, 3)
    return view.reshape(rows * cols // LANES, LANES)


def on_device(a_blocks, b_blocks, c_blocks, stack_a, stack_b, stack_c, stack_len):
    hbm = pl.BlockSpec(memory_space=pl.ANY)
    panel = pltpu.VMEM((1024, LANES), F32)
    split = pltpu.VMEM((32, BLK, LANES), BF16)
    dma, flag = pltpu.SemaphoreType.DMA, pltpu.SemaphoreType.REGULAR
    picks = pltpu.SMEM(stack_a.shape, jnp.int32)
    return pl.pallas_call(
        kernel,
        out_shape=pltpu.VMEM(c_blocks.shape, F32),
        in_specs=[hbm] * 7,
        out_specs=pl.BlockSpec(memory_space=pltpu.VMEM),
        scratch_shapes=[
            panel, panel, panel, panel, panel, panel, pltpu.VMEM((256, LANES), F32), pltpu.VMEM((512, LANES), F32),
            split, split, split, split,
            pltpu.VMEM((SUB, BLK, LANES), F32), pltpu.VMEM((4096, LANES), F32), pltpu.VMEM((BLK, 2 * LANES), F32),
            picks, picks, pltpu.SMEM(stack_len.shape[::-1], jnp.int32), pltpu.VMEM(stack_c.shape, jnp.int32),
            dma((7,)), dma((4, 2)), dma((4, 2)), dma((4,)), dma((4,)), dma((4,)), dma((4,)), dma((4,)), dma((4,)),
            dma((4, 2)), dma((2,)), dma((2,)), dma((3,)), dma((2,)), dma((3,)), flag, flag,
        ],
        compiler_params=pltpu.CompilerParams(collective_id=0, has_side_effects=True, vmem_limit_bytes=56 * 2 ** 20),
        cost_estimate=pl.CostEstimate(flops=300_000_000, bytes_accessed=4_000_000, transcendentals=0),
    )(stack_a, stack_b, stack_len.T, stack_c, tiles(a_blocks), tiles(b_blocks), c_blocks)


def solution(mesh):
    placed = P("row", "col")
    return jax.shard_map(
        on_device, mesh=mesh, in_specs=(placed,) * 7, out_specs=placed, check_vma=False
    )
```

```python
import functools

import jax
import jax.numpy as jnp
from jax import lax
from jax.experimental import pallas as pl
from jax.experimental.pallas import tpu as pltpu
from jax.sharding import PartitionSpec as P

MESH = pl.DeviceIdType.MESH
NX, NY, NZL, NZH = 4, 4, 8, 4
BLK = 64
LANES = 128
SUB = 8
PARTS = 4
F32, BF16 = jnp.float32, jnp.bfloat16


def on_left():
    return lax.broadcasted_iota(jnp.int32, (32, LANES), 1) < BLK


def halves(block):
    high = block.astype(BF16).astype(F32)
    rest = block - high
    left = on_left()
    even = jnp.where(left, high, pltpu.roll(rest, BLK, 1))
    odd = jnp.where(left, pltpu.roll(high, BLK, 1), rest)
    return even, odd


def split_a(panel, out, part):
    for s in range(SUB):
        even, odd = halves(panel[pl.ds(part * 256 + s, 32, stride=SUB), :])
        out[part * SUB + s, 0:32, :] = even.astype(BF16)
        out[part * SUB + s, 32:64, :] = odd.astype(BF16)


def split_b(panel, out, mixed, part):
    for s in range(SUB):
        even, odd = halves(panel[pl.ds(part * 256 + s, 32, stride=SUB), :])
        mixed[s, pl.ds(0, 32, stride=2), :] = even
        mixed[s, pl.ds(1, 32, stride=2), :] = odd
        out[part * SUB + s] = mixed[s].astype(BF16)


def multiply(phase, first, wide, sa_ref, sb_ref, fa, fb, prods):
    left = on_left()

    def body(h, carry):
        for n in range(wide * SUB):
            g, s = h * wide + n // SUB, n % SUB
            e = g * SUB + s
            a = fa[sa_ref[phase, e]]
            b = fb[sb_ref[phase, e]]
            both = jnp.dot(a, jnp.concatenate([b, b], axis=0), preferred_element_type=F32)
            whole = both + pltpu.roll(both, BLK, 1)
            prods[pl.ds(first + g * 256 + s, 32, stride=SUB), :] = jnp.where(left, whole[0:32], whole[32:64])
        return carry

    lax.fori_loop(0, 8 // wide, body, 0)


def spread(prods, groups, wide, spots, acc):
    def body(h, carry):
        for u in range(wide):
            t = h * wide + u
            rows = [prods[pl.ds(g * 256 + t * SUB, SUB), :] for g in range(groups)]
            x = jnp.concatenate(rows, axis=0)
            high = x.astype(BF16)
            rest = (x - high.astype(F32)).astype(BF16)
            add = jnp.dot(spots, jnp.concatenate([high, rest], axis=0), preferred_element_type=F32)
            at = pl.ds(pl.multiple_of(t * LANES, LANES), LANES)
            acc[:, at] = acc[:, at] + add
        return carry

    lax.fori_loop(0, 32 // wide, body, 0)


def kernel(sa_hbm, sb_hbm, sl_hbm, sc_hbm, a_hbm, b_hbm, c_hbm, acc,
           a_own, b_own, a_next, a_side, b_one, b_two, a_relay, b_relay, fa, fb, fa_two, fb_two, mixed, prods, spot,
           sa_ref, sb_ref, sl_ref, sc_ref,
           own_sem, a_send, a_recv, side_send, side_recv, b_send, b_recv, b2_send, b2_recv,
           rel_send, rel_recv, far_send, brel_send, brel_recv, bfar_send, far_ok, wrap_ok):
    row, col = lax.axis_index("row"), lax.axis_index("col")
    x, zl = lax.rem(row, NX), lax.div(row, NX)
    core, y, zh = lax.rem(col, 2), lax.rem(lax.div(col, 2), NY), lax.div(col, 2 * NY)

    def at(y_, zh_):
        return (row, (lax.rem(zh_ + NZH, NZH) * NY + y_) * 2 + core)

    def beside(x_, zl_):
        return (lax.rem(zl_ + NZL, NZL) * NX + x_, col)

    other = (row, col + 1 - 2 * core)
    far = at(3, zh - 1)
    above3, above2 = beside(3, zl - 1), beside(2, zl - 1)
    far_asks = (zh == 0) | (zh == NZH - 1)
    far_answers = (y == 3) & (zh >= NZH - 2)
    wrap_asks = zl == 0
    wrap_last = zl == NZL - 1

    sources = (sa_hbm, sb_hbm, sl_hbm, sc_hbm, a_hbm, b_hbm, c_hbm)
    places = (sa_ref, sb_ref, sl_ref, sc_ref, a_own, b_own, acc)
    own = [pltpu.make_async_copy(s_, d_, own_sem.at[n]) for n, (s_, d_) in enumerate(zip(sources, places))]

    barrier = pltpu.get_barrier_semaphore()

    def greet(device):
        pl.semaphore_signal(barrier, inc=1, device_id=device, device_id_type=MESH)

    @pl.when(far_asks)
    def _():
        greet(far)

    @pl.when(wrap_asks)
    def _():
        greet(above3)

        @pl.when(x != 1)
        def _():
            greet(above2)

    @pl.when((y == 3) & (zh < NZH - 2))
    def _():
        for k in range(NY):
            greet(at(k, zh + 1))

    @pl.when(y >= 1)
    def _():
        greet(at(0, zh))

    @pl.when(y <= 2)
    def _():
        greet(at(y + 1, zh))

    greet(other)

    for here, there in ((0, (1, 2)), (1, (2, 3)), (2, (3, 0, 1)), (3, (0,))):
        @pl.when(x == here)
        def _():
            for k in there:
                greet(beside(k, zl))

    for here, there in ((2, (0, 2, 3)), (3, (0, 1, 2, 3))):
        @pl.when((x == here) & jnp.logical_not(wrap_last))
        def _():
            for k in there:
                greet(beside(k, zl + 1))

    for copy in own[4:6] + own[:4] + own[6:]:
        copy.start()

    expected = (jnp.where(y == 0, 4, 2) + 2 + jnp.where(wrap_asks, 0, jnp.where(x == 1, 1, 2))
                + jnp.where(far_asks, 0, 1) + jnp.where(far_answers, NY, 0)
                + jnp.where(wrap_last, jnp.where(x == 3, 4, jnp.where(x == 2, 3, 0)), 0))
    pl.semaphore_wait(barrier, expected)

    @pl.when(far_answers)
    def _():
        for k in range(NY):
            pl.semaphore_signal(far_ok, inc=1, device_id=at(k, zh + 1), device_id_type=MESH)

    for here, there in ((2, (0, 2, 3)), (3, (0, 1, 2, 3))):
        @pl.when((x == here) & wrap_last)
        def _():
            for k in there:
                pl.semaphore_signal(wrap_ok, inc=1, device_id=beside(k, zl + 1), device_id_type=MESH)

    def quarter(ref, q):
        return ref.at[pl.ds(q * 256, 256)]

    def half(ref, q, h):
        return ref.at[pl.ds(q * 256 + h * 128, 128)]

    def send(source, target, send_sem, recv_sem, device):
        return pltpu.make_async_remote_copy(source, target, send_sem, recv_sem, device_id=device, device_id_type=MESH)

    def a_copy(q, h, device):
        return send(half(a_hbm, q, h), half(a_next, q, h), a_send.at[q, h], a_recv.at[q, h], device)

    def relay_copy(q, h):
        return send(half(a_hbm, q, h), half(a_relay, 0, h), rel_send.at[q, h], rel_recv.at[h], at(q, zh))

    def far_copy(q, h):
        return send(half(a_relay, 0, h), half(a_next, q, h), far_send.at[h], a_recv.at[q, h], far)

    def side_copy(q, source):
        return send(quarter(source, q), quarter(a_side, q), side_send.at[q], side_recv.at[q], other)

    def b_copy(q, device):
        return send(quarter(b_hbm, q), quarter(b_one, q), b_send.at[q], b_recv.at[q], device)

    def b2_copy(q, device):
        return send(quarter(b_hbm, q), quarter(b_two, q), b2_send.at[q], b2_recv.at[q], device)

    def b_relay_copy(q, slot, sem, device):
        return send(quarter(b_hbm, q), quarter(b_relay, slot), brel_send.at[sem], brel_recv.at[slot], device)

    def b_far_copy(sem, slot, q, target, recv, device):
        return send(quarter(b_relay, slot), quarter(target, q), bfar_send.at[sem], recv.at[q], device)

    @pl.when(y == 0)
    def _():
        for q in (2, 1, 3):
            for h in range(2):
                relay_copy(q, h).start()

    def send_above():
        @pl.when(x == 0)
        def _():
            b_copy(0, above3).start()
            b_copy(1, above3).start()
            b2_copy(0, above2).start()

        @pl.when(x == 1)
        def _():
            for q in range(3):
                b2_copy(q, above3).start()

    @pl.when(x == 0)
    def _():
        b_relay_copy(2, 1, 1, beside(3, zl)).start()
        b_relay_copy(3, 0, 2, beside(2, zl)).start()
        b_relay_copy(1, 0, 0, beside(3, zl)).start()

    @pl.when(x == 1)
    def _():
        b_relay_copy(3, 1, 0, beside(2, zl)).start()

    def far_start():
        @pl.when(far_asks)
        def _():
            pl.semaphore_wait(far_ok, 1)

        @pl.when(y == 0)
        def _():
            for h in range(2):
                a_copy(0, h, far).start()

        for q in range(1, PARTS):
            @pl.when(y == q)
            def _():
                for h in range(2):
                    relay_copy(q, h).wait_recv()
                    far_copy(q, h).start()

    @pl.when(jnp.logical_not(far_asks))
    def _():
        far_start()

    @pl.when(y >= 1)
    def _():
        for q in range(PARTS):
            for h in range(2):
                a_copy(q, h, at(y - 1, zh)).start()

    @pl.when(x >= 1)
    def _():
        for q in range(PARTS):
            b_copy(q, beside(x - 1, zl)).start()

    @pl.when(core == 1)
    def _():
        for q in range(PARTS):
            side_copy(q, a_hbm).start()

    def forward_above():
        @pl.when(x == 2)
        def _():
            b_relay_copy(3, 0, 0, above3).wait_recv()
            b_far_copy(0, 0, 3, b_one, b_recv, above3).start()
            b_far_copy(1, 0, 3, b_two, b2_recv, above2).start()
            b_relay_copy(3, 1, 0, above3).wait_recv()
            b_far_copy(2, 1, 3, b_two, b2_recv, above3).start()

        @pl.when(x == 3)
        def _():
            b_relay_copy(2, 1, 0, above3).wait_recv()
            b_far_copy(1, 1, 2, b_one, b_recv, above3).start()
            b_far_copy(2, 1, 2, b_two, b2_recv, above2).start()
            b_relay_copy(1, 0, 0, above3).wait_recv()
            b_far_copy(0, 0, 1, b_two, b2_recv, above2).start()

    def far_left():
        @pl.when(y == 0)
        def _():
            for h in range(2):
                a_copy(0, h, far).wait_send()

        @pl.when(y >= 1)
        def _():
            for h in range(2):
                far_copy(1, h).wait_send()

    def mark(phase, at_):
        slot = lax.broadcasted_iota(jnp.int32, (BLK, BLK), 0)
        entry = lax.broadcasted_iota(jnp.int32, (BLK, BLK), 1)
        hit = (slot == sc_ref[phase:phase + 1, :]) & (entry < sl_ref[0, phase])
        ones = jnp.where(hit, 1.0, 0.0)
        spot[:, at_:at_ + BLK] = ones

    own[4].wait()
    for q in range(PARTS):
        split_a(a_own, fa, q)
    own[5].wait()
    for q in range(PARTS):
        split_b(b_own, fb, mixed, q)

    for copy in own[:4]:
        copy.wait()
    mark(0, 0)
    mark(0, BLK)
    multiply(0, 0, 1, sa_ref, sb_ref, fa, fb, prods)
    own[6].wait()
    spread(prods, 8, 4, spot[:, 0:LANES].astype(BF16), acc)

    @pl.when(wrap_asks)
    def _():
        pl.semaphore_wait(wrap_ok, jnp.where(x == 1, 1, 2))

    send_above()
    forward_above()

    @pl.when(x >= 2)
    def _():
        for q in range(PARTS):
            b2_copy(q, beside(x - 2, zl)).start()

    @pl.when(far_asks)
    def _():
        far_start()


    for n in range(2):
        mark(1, n * LANES)
        mark(2, n * LANES + BLK)
    for q in range(PARTS):
        b_copy(q, other).wait_recv()
        split_b(b_one, fb, mixed, q)

    def phase_one():
        for q in range(PARTS):
            side_copy(q, a_hbm).wait_recv()
            split_a(a_side, fa, q)
        multiply(1, 0, 8, sa_ref, sb_ref, fa, fb, prods)

    @pl.when(core == 0)
    def _():
        phase_one()

    for q in range(PARTS):
        b2_copy(q, other).wait_recv()
        split_b(b_two, fb_two, mixed, q)
    for q in range(PARTS):
        for h in range(2):
            a_copy(q, h, far).wait_recv()

        @pl.when(core == 0)
        def _():
            side_copy(q, a_next).start()

        split_a(a_next, fa_two, q)
    multiply(2, 2048, 8, sa_ref, sb_ref, fa_two, fb_two, prods)

    @pl.when(core == 1)
    def _():
        phase_one()

    spread(prods, 16, 32, spot[...].astype(BF16), acc)

    far_left()

    for q in range(PARTS):
        side_copy(q, a_hbm).wait_send()

    @pl.when(y == 0)
    def _():
        for q in (1, 2, 3):
            for h in range(2):
                relay_copy(q, h).wait_send()

    @pl.when(y >= 1)
    def _():
        for q in range(PARTS):
            for h in range(2):
                a_copy(q, h, far).wait_send()

    @pl.when(x == 0)
    def _():
        b_copy(0, other).wait_send()
        b_copy(1, other).wait_send()
        b2_copy(0, other).wait_send()
        for sem in range(3):
            b_relay_copy(0, 0, sem, other).wait_send()

    @pl.when(x >= 1)
    def _():
        for q in range(PARTS):
            b_copy(q, other).wait_send()
        for q in range(3):
            b2_copy(q, other).wait_send()

    @pl.when(x == 1)
    def _():
        b_relay_copy(0, 0, 0, other).wait_send()

    @pl.when(x >= 2)
    def _():
        b2_copy(3, other).wait_send()
        for sem in range(3):
            b_far_copy(sem, 0, 0, b_one, b_recv, other).wait_send()


def tiles(panel):
    rows, cols = panel.shape
    view = panel.reshape(rows // SUB, SUB, cols // LANES, LANES).transpose(0, 2, 1, 3)
    return view.reshape(rows * cols // LANES, LANES)


def on_device(a_blocks, b_blocks, c_blocks, stack_a, stack_b, stack_c, stack_len):
    hbm = pl.BlockSpec(memory_space=pl.ANY)
    panel = pltpu.VMEM((1024, LANES), F32)
    split = pltpu.VMEM((32, BLK, LANES), BF16)
    dma, flag = pltpu.SemaphoreType.DMA, pltpu.SemaphoreType.REGULAR
    picks = pltpu.SMEM(stack_a.shape, jnp.int32)
    return pl.pallas_call(
        kernel,
        out_shape=pltpu.VMEM(c_blocks.shape, F32),
        in_specs=[hbm] * 7,
        out_specs=pl.BlockSpec(memory_space=pltpu.VMEM),
        scratch_shapes=[
            panel, panel, panel, panel, panel, panel, pltpu.VMEM((256, LANES), F32), pltpu.VMEM((512, LANES), F32),
            split, split, split, split,
            pltpu.VMEM((SUB, BLK, LANES), F32), pltpu.VMEM((4096, LANES), F32), pltpu.VMEM((BLK, 2 * LANES), F32),
            picks, picks, pltpu.SMEM(stack_len.shape[::-1], jnp.int32), pltpu.VMEM(stack_c.shape, jnp.int32),
            dma((7,)), dma((4, 2)), dma((4, 2)), dma((4,)), dma((4,)), dma((4,)), dma((4,)), dma((4,)), dma((4,)),
            dma((4, 2)), dma((2,)), dma((2,)), dma((3,)), dma((2,)), dma((3,)), flag, flag,
        ],
        compiler_params=pltpu.CompilerParams(collective_id=0, has_side_effects=True, vmem_limit_bytes=56 * 2 ** 20),
        cost_estimate=pl.CostEstimate(flops=300_000_000, bytes_accessed=4_000_000, transcendentals=0),
    )(stack_a, stack_b, stack_len.T, stack_c, tiles(a_blocks), tiles(b_blocks), c_blocks)


def solution(mesh):
    placed = P("row", "col")
    return jax.shard_map(
        on_device, mesh=mesh, in_specs=(placed,) * 7, out_specs=placed, check_vma=False
    )
```
